256 devices in a mesh: sec: 16 (over x_hi, y, core), seq: 16 (over z, x_lo).
Axes of the slice: x: 4 (x_hi: 2, x_lo: 2; x = x_hi * 2 + x_lo), y: 4, z: 8, core: 2. Of those that a mesh axis runs over, the one named last changes fastest.
Arguments:
- stream: bfloat16 [512, 2048], replicated, may hold values from -6 to 6
- norm_gain: float32 [16, 2048], P('sec'), may hold values from 0.1 to 1.9
- qkv_weight: bfloat16 [16, 2048, 6144], P('sec', None, 'seq'), may hold values from -0.125 to 0.125
- out_weight: bfloat16 [16, 2048, 2048], P('sec', 'seq'), may hold values from -0.375 to 0.375
- stale_kv: bfloat16 [16, 512, 16, 256], P('sec', None, 'seq'), may hold values from -128 to 128, as said below
Outputs:
- section_out: bfloat16 [16, 512, 2048], P('sec', 'seq')
- fresh_kv: bfloat16 [16, 512, 16, 256], P('sec', None, 'seq')
The draws below stay inside these ranges and needn't reach their ends.
Inputs may be any that keep to these rules, and one draw needn't show every extreme that they name: `stale_kv`: the last 128 entries of each head (values) are of order one; keys may carry a larger scale per token.
All inputs are finite; a program needn't handle non-finite values.
Results may differ from the reference program's by a relative error of at most 0.04.
Values may be sent and summed in bfloat16 or wider, within the bound.
A program may use at most 64 MiB of HBM per device.

```python
import math
import jax
import jax.numpy as jnp
from jax import lax

HEADS = 16
HD = 128
PATCHES = 4
ROWS = 8
WIDTH = 2048
TOKENS = 512
SECTIONS = 16
N_SEC = 16
N_SEQ = 16


def draw_stale_kv(key, part):
    shape = (N_SEC, TOKENS, HEADS, 2 * HD)
    first_key = jax.random.fold_in(jax.random.fold_in(key, 11), 0)
    values = jax.random.truncated_normal(first_key, -4.0, 4.0, shape, jnp.float32)
    return values.astype(jnp.bfloat16)


def block_scale(rng, extent, cuts, least, top_value):
    loudness, own = 1.0, jax.random.fold_in(rng, 6)
    for position, shards_of in cuts:
        steps = jnp.exp(jax.random.uniform(jax.random.fold_in(own, position), (shards_of,), jnp.float32, least / len(cuts), top_value / len(cuts)))
        loudness = loudness * jnp.repeat(steps, extent[position] // shards_of).reshape([-1 if axis == position else 1 for axis in range(len(extent))])
    return loudness


def scatter_about(key, extent, scale, reach, shards=(), kind=jnp.bfloat16):
    gain = block_scale(key, extent, shards, -0.22, 0.18) if shards else 1.0
    result = jax.random.normal(key, extent, jnp.float32) * scale * gain
    return jnp.minimum(jnp.maximum(result, -reach), reach).astype(kind)


def setup_inputs(seed: int = 0) -> dict:
    arg_keys = jax.random.split(jax.random.key(seed), 6)
    return {
        "stream": scatter_about(arg_keys[0], (TOKENS, WIDTH), 1.0, 6.0),
        "norm_gain": jnp.clip(1.0 + 0.18 * jax.random.normal(arg_keys[1], (SECTIONS, WIDTH), jnp.float32), 0.1, 1.9),
        "qkv_weight": scatter_about(arg_keys[2], (SECTIONS, WIDTH, 3 * WIDTH), WIDTH ** -0.5, 0.125, ((0, 16), (2, 16))),
        "out_weight": scatter_about(arg_keys[3], (SECTIONS, WIDTH, WIDTH), (2 * HD) ** -0.5, 0.375, ((0, 16), (1, 16))),
        "stale_kv": draw_stale_kv(jax.random.fold_in(arg_keys[5], 71), 0),
    }


def reference(stream, norm_gain, qkv_weight, out_weight, stale_kv):
    width = HEADS * HD
    share = HEADS // N_SEQ
    scale = 1.0 / math.sqrt(HD)
    x_all = stream.reshape(N_SEQ, PATCHES, ROWS, width)
    patch_ids = jnp.arange(PATCHES)
    same_shard = jnp.eye(N_SEQ, dtype=bool)
    outs = []
    kv_list = []
    for section in range(N_SEC):
        stale = stale_kv[section].reshape(N_SEQ, PATCHES, ROWS, HEADS, 2 * HD)
        stale_keys = stale[..., :HD].astype(jnp.float32)
        stale_vals = stale[..., HD:].astype(jnp.float32)
        fresh = jnp.zeros_like(stale)
        w_out = out_weight[section].reshape(N_SEQ, share * HD, width).astype(jnp.float32)
        pieces = []
        for patch in range(PATCHES):
            x_rows = x_all[:, patch]
            x_float = x_rows.astype(jnp.float32)
            meansq = lax.optimization_barrier(jnp.mean(x_float * x_float, axis=-1, keepdims=True))
            normed = (x_float * lax.rsqrt(meansq + 1e-06) * norm_gain[section]).astype(jnp.bfloat16)
            normed = normed.reshape(N_SEQ * ROWS, width)
            projected = jnp.dot(normed, qkv_weight[section], preferred_element_type=jnp.float32).astype(jnp.bfloat16)
            projected = projected.reshape(N_SEQ, ROWS, HEADS, 3, HD)
            query = projected[..., 0, :].astype(jnp.float32)
            kv_new = jnp.concatenate([projected[..., 1, :], projected[..., 2, :]], axis=-1)
            fresh = fresh.at[:, patch].set(kv_new)
            fresh_keys = fresh[..., :HD].astype(jnp.float32)
            fresh_vals = fresh[..., HD:].astype(jnp.float32)
            key_mask = same_shard[:, :, None] & (patch_ids <= patch)[None, None, :]
            wide_mask = key_mask[:, None, None, :, :, None]
            s_stale = jnp.einsum('irhd,jpkhd->irhjpk', query, stale_keys) * scale
            s_fresh = jnp.einsum('irhd,jpkhd->irhjpk', query, fresh_keys) * scale
            scores = jnp.where(wide_mask, s_fresh, s_stale)
            peak = lax.optimization_barrier(jnp.max(scores, axis=(3, 4, 5)))
            expo = jnp.exp(scores - peak[..., None, None, None])
            total = lax.optimization_barrier(jnp.sum(expo, axis=(3, 4, 5)))
            weights = (expo / total[..., None, None, None]).astype(jnp.bfloat16).astype(jnp.float32)
            context = jnp.einsum('irhjpk,jpkhd->irhd', jnp.where(wide_mask, weights, 0.0), fresh_vals)
            context = context + jnp.einsum('irhjpk,jpkhd->irhd', jnp.where(wide_mask, 0.0, weights), stale_vals)
            context = context.astype(jnp.bfloat16).astype(jnp.float32).reshape(N_SEQ, ROWS, N_SEQ, share * HD)
            partial_rows = jnp.einsum('irgc,gcw->girw', context, w_out).astype(jnp.bfloat16)
            partial_rows = lax.optimization_barrier(partial_rows).astype(jnp.float32)
            summed = lax.optimization_barrier(jnp.sum(partial_rows, axis=0))
            pieces.append((summed + x_float).astype(jnp.bfloat16))
        x_all = jnp.stack(pieces, axis=1)
        outs.append(x_all.reshape(TOKENS, width))
        kv_list.append(fresh.reshape(TOKENS, HEADS, 2 * HD))
    return (jnp.stack(outs), jnp.stack(kv_list))
```

```python
import functools
import math

import jax
import jax.numpy as jnp
from jax import lax
from jax.experimental import pallas as pl
from jax.experimental.pallas import tpu as pltpu
from jax.sharding import PartitionSpec as P

MESH = pl.DeviceIdType.MESH
SECS = 16
RING = 8
SEQS = 16
PATCHES = 4
ROWS = 8
SHARD = PATCHES * ROWS
CHUNK = 128
CHUNKS = 4
PER_CHUNK = CHUNK // SHARD
HEAD = 128
TILE = 256
EPS = 1e-06

GATHER = (
    ((1, 0), (0, 0)),
    ((-1, 0), (0, 0)),
    ((0, 1), (0, 0)),
    ((1, 0), (-1, 0)),
    ((-1, 0), (1, 0)),
    ((0, 1), (1, 0)),
    ((1, 0), (-2, 0)),
    ((-1, 0), (2, 0)),
    ((0, 1), (2, 0)),
    ((1, 0), (-3, 0)),
    ((-1, 0), (2, 1)),
    ((0, 1), (-2, 0)),
    ((1, 0), (-2, 1)),
    ((-1, 0), (3, 1)),
    ((0, 1), (-1, 0)),
)
Z_ORDER = (4, 3, -3, 2, -2, 1, -1, 0)


def slot(dz, dx):
    return (dz % RING) * 2 + dx % 2


def kernel(
    stream_ref,
    gain_ref,
    wqkv_ref,
    wout_ref,
    stale_ref,
    out_ref,
    fresh_ref,
    wfull,
    wqkv,
    gain,
    stale,
    ctx_in,
    x_in,
    x_cur,
    ctx_out,
    fresh,
    fin_in,
    fin_x,
    fin_out,
    load_sem,
    w_send,
    w_recv,
    own_send,
    ctx_send,
    ctx_recv,
    x_send,
    x_recv,
    fin_recv,
    finx_recv,
    out_send,
    out_recv,
    fresh_sem,
):
    s = lax.axis_index("sec")
    j = lax.axis_index("seq")
    z = j // 2
    xl = j % 2
    ahead = (s + 1) % SECS
    behind = (s + SECS - 1) % SECS
    width = wfull.shape[1]

    def place(dz, dx):
        return ((z + dz + RING) % RING) * 2 + (xl + dx) % 2

    loads = [
        pltpu.make_async_copy(wqkv_ref.at[0], wqkv, load_sem.at[0]),
        pltpu.make_async_copy(gain_ref, gain, load_sem.at[1]),
        pltpu.make_async_copy(stale_ref, stale, load_sem.at[2]),
    ]
    for load in loads:
        load.start()
    stream_load = pltpu.make_async_copy(stream_ref, x_cur, load_sem.at[3])

    @pl.when(s == 0)
    def _():
        stream_load.start()

    barrier = pltpu.get_barrier_semaphore()

    def greet(i, carry):
        pl.semaphore_signal(barrier, inc=1, device_id=(ahead, i), device_id_type=MESH)
        pl.semaphore_signal(barrier, inc=1, device_id=(behind, i), device_id_type=MESH)
        return carry

    lax.fori_loop(0, SEQS, greet, 0)
    for dz, dx in ((1, 0), (-1, 0), (0, 1)):
        pl.semaphore_signal(barrier, inc=1, device_id=(s, place(dz, dx)), device_id_type=MESH)
    pl.semaphore_wait(barrier, 2 * SEQS + 3)

    def block(index):
        return pl.ds(pl.multiple_of(index * HEAD, HEAD), HEAD)

    own = pltpu.make_async_remote_copy(
        src_ref=wout_ref.at[0],
        dst_ref=wfull.at[block(j), :],
        send_sem=own_send,
        recv_sem=w_recv.at[0],
        device_id=(ahead, j),
        device_id_type=MESH,
    )
    own.start()

    def wait_block(dz, dx):
        rows = block(place(dz, dx))
        pltpu.make_async_copy(
            wfull.at[rows, :], wfull.at[rows, :], w_recv.at[slot(dz, dx)]
        ).wait()

    def gather():
        arrived = set()

        def need(rel):
            if slot(*rel) not in arrived:
                arrived.add(slot(*rel))
                wait_block(*rel)

        sends = []
        for index, (step, rel) in enumerate(GATHER):
            need(rel)
            rows = block(place(*rel))
            send = pltpu.make_async_remote_copy(
                src_ref=wfull.at[rows, :],
                dst_ref=wfull.at[rows, :],
                send_sem=w_send.at[index],
                recv_sem=w_recv.at[slot(rel[0] - step[0], rel[1] + step[1])],
                device_id=(s, place(*step)),
                device_id_type=MESH,
            )
            send.start()
            sends.append(send)
        for dz in range(RING):
            for dx in range(2):
                need((dz, dx))
        for send in sends:
            send.wait_send()

    pl.when(s != 0)(gather)
    for load in loads:
        load.wait()

    @pl.when(s == 0)
    def _():
        stream_load.wait()

    scale = 1.0 / math.sqrt(HEAD)

    def wait_bytes(ref, sem):
        pltpu.make_async_copy(ref, ref, sem).wait()

    def process(c, carry):
        @pl.when(s != 0)
        def _():
            wait_bytes(ctx_in.at[c], ctx_recv.at[c])
            wait_bytes(x_in.at[c], x_recv.at[c])

            def columns(n, carry):
                cols = pl.ds(pl.multiple_of(n * TILE, TILE), TILE)
                lhs = jnp.concatenate([ctx_in[c, g] for g in range(SEQS)], axis=1)
                total = jnp.dot(lhs, wfull[:, cols], preferred_element_type=jnp.float32)
                total = total + x_in[c, :, cols].astype(jnp.float32)
                x_cur[c, :, cols] = total.astype(jnp.bfloat16)
                return carry

            lax.fori_loop(0, width // TILE, columns, 0)

        @pl.when(s != SECS - 1)
        def _():
            pltpu.make_async_remote_copy(
                src_ref=x_cur.at[c],
                dst_ref=x_in.at[c],
                send_sem=x_send.at[c],
                recv_sem=x_recv.at[c],
                device_id=(ahead, j),
                device_id_type=MESH,
            ).start()

        mine = c == j // PER_CHUNK
        my_rows = pl.ds(pl.multiple_of((j % PER_CHUNK) * SHARD, SHARD), SHARD)

        @pl.when(mine & (s == SECS - 1))
        def _():
            pltpu.make_async_remote_copy(
                src_ref=x_cur.at[c, my_rows, :],
                dst_ref=fin_x,
                send_sem=x_send.at[0],
                recv_sem=finx_recv,
                device_id=(ahead, j),
                device_id_type=MESH,
            ).start()

        @pl.when(mine & (s != 0))
        def _():
            pltpu.make_async_remote_copy(
                src_ref=x_cur.at[c, my_rows, :],
                dst_ref=out_ref.at[0],
                send_sem=out_send,
                recv_sem=out_recv,
                device_id=(behind, j),
                device_id_type=MESH,
            ).start()

        x = x_cur[c].astype(jnp.float32)
        meansq = jnp.mean(x * x, axis=-1, keepdims=True)
        normed = (x * lax.rsqrt(meansq + EPS) * gain[...]).astype(jnp.bfloat16)
        qkv = jnp.dot(normed, wqkv[...], preferred_element_type=jnp.float32).astype(jnp.bfloat16)
        query = qkv[:, :HEAD]
        key = qkv[:, HEAD : 2 * HEAD]
        value = qkv[:, 2 * HEAD :]
        tokens = pl.ds(pl.multiple_of(c * CHUNK, CHUNK), CHUNK)
        fresh[tokens, :] = qkv[:, HEAD:]
        pltpu.make_async_copy(
            fresh.at[tokens, :], fresh_ref.at[tokens, :], fresh_sem.at[c]
        ).start()

        contract = (((1,), (1,)), ((), ()))
        s_stale = (
            lax.dot_general(
                query, stale[:, :HEAD], contract, preferred_element_type=jnp.float32
            )
            * scale
        )
        s_fresh = (
            lax.dot_general(query, key, contract, preferred_element_type=jnp.float32) * scale
        )
        tokens_all = stale.shape[0]

        def is_fresh(count, first):
            row = lax.broadcasted_iota(jnp.int32, (CHUNK, count), 0) + c * CHUNK
            col = lax.broadcasted_iota(jnp.int32, (CHUNK, count), 1) + first
            same = (row >> 5) == (col >> 5)
            return same & (((col & 31) >> 3) <= ((row & 31) >> 3))

        low = -1e30
        s_stale = jnp.where(is_fresh(tokens_all, 0), low, s_stale)
        s_fresh = jnp.where(is_fresh(CHUNK, c * CHUNK), s_fresh, low)
        peak = jnp.maximum(
            jnp.max(s_stale, axis=1, keepdims=True), jnp.max(s_fresh, axis=1, keepdims=True)
        )
        e_stale = jnp.exp(s_stale - peak)
        e_fresh = jnp.exp(s_fresh - peak)
        norm = 1.0 / (
            jnp.sum(e_stale, axis=1, keepdims=True) + jnp.sum(e_fresh, axis=1, keepdims=True)
        )
        w_stale = (e_stale * norm).astype(jnp.bfloat16)
        w_fresh = (e_fresh * norm).astype(jnp.bfloat16)
        context = jnp.dot(w_stale, stale[:, HEAD:], preferred_element_type=jnp.float32)
        context = context + jnp.dot(w_fresh, value, preferred_element_type=jnp.float32)
        ctx_out[c] = context.astype(jnp.bfloat16)

        @pl.when(s != SECS - 1)
        def _():
            for dz in Z_ORDER:
                for dx in (1, 0):
                    pltpu.make_async_remote_copy(
                        src_ref=ctx_out.at[c],
                        dst_ref=ctx_in.at[c, j],
                        send_sem=ctx_send.at[c],
                        recv_sem=ctx_recv.at[c],
                        device_id=(ahead, place(dz, dx)),
                        device_id_type=MESH,
                    ).start()

        @pl.when(s == SECS - 1)
        def _():
            for i in range(PER_CHUNK):
                pltpu.make_async_remote_copy(
                    src_ref=ctx_out.at[c, pl.ds(i * SHARD, SHARD), :],
                    dst_ref=fin_in.at[j],
                    send_sem=ctx_send.at[c],
                    recv_sem=fin_recv,
                    device_id=(ahead, c * PER_CHUNK + i),
                    device_id_type=MESH,
                ).start()

        return carry

    lax.fori_loop(0, CHUNKS, process, 0)

    @pl.when(s == 0)
    def _():
        gather()
        wait_bytes(fin_in, fin_recv)
        wait_bytes(fin_x, finx_recv)

        def columns(n, carry):
            cols = pl.ds(pl.multiple_of(n * TILE, TILE), TILE)
            lhs = jnp.concatenate([fin_in[g] for g in range(SEQS)], axis=1)
            total = jnp.dot(lhs, wfull[:, cols], preferred_element_type=jnp.float32)
            total = total + fin_x[:, cols].astype(jnp.float32)
            fin_out[:, cols] = total.astype(jnp.bfloat16)
            return carry

        lax.fori_loop(0, width // TILE, columns, 0)
        pltpu.make_async_remote_copy(
            src_ref=fin_out,
            dst_ref=out_ref.at[0],
            send_sem=out_send,
            recv_sem=out_recv,
            device_id=(behind, j),
            device_id_type=MESH,
        ).start()

    own.wait_send()

    def drain(c, carry):
        tokens = pl.ds(pl.multiple_of(c * CHUNK, CHUNK), CHUNK)
        pltpu.make_async_copy(
            fresh.at[tokens, :], fresh_ref.at[tokens, :], fresh_sem.at[c]
        ).wait()

        @pl.when(s != SECS - 1)
        def _():
            wait_bytes(ctx_in.at[c], ctx_send.at[c])
            wait_bytes(x_in.at[c], x_send.at[c])

        @pl.when(s == SECS - 1)
        def _():
            wait_bytes(ctx_out.at[c], ctx_send.at[c])

        return carry

    lax.fori_loop(0, CHUNKS, drain, 0)

    @pl.when(s == SECS - 1)
    def _():
        wait_bytes(fin_x, x_send.at[0])

    wait_bytes(fin_out, out_send)
    wait_bytes(out_ref.at[0], out_recv)


def on_device(stream, norm_gain, qkv_weight, out_weight, stale_kv):
    tokens, width = stream.shape
    stale = stale_kv.reshape(tokens, 2 * HEAD)
    any_spec = pl.BlockSpec(memory_space=pl.ANY)
    bf16 = jnp.bfloat16
    dma = pltpu.SemaphoreType.DMA
    out, fresh = pl.pallas_call(
        kernel,
        out_shape=(
            jax.ShapeDtypeStruct((1, SHARD, width), bf16),
            jax.ShapeDtypeStruct((tokens, 2 * HEAD), bf16),
        ),
        in_specs=[any_spec] * 5,
        out_specs=(any_spec, any_spec),
        scratch_shapes=[
            pltpu.VMEM((width, width), bf16),
            pltpu.VMEM((width, 3 * HEAD), bf16),
            pltpu.VMEM((1, width), jnp.float32),
            pltpu.VMEM((tokens, 2 * HEAD), bf16),
            pltpu.VMEM((CHUNKS, SEQS, CHUNK, HEAD), bf16),
            pltpu.VMEM((CHUNKS, CHUNK, width), bf16),
            pltpu.VMEM((CHUNKS, CHUNK, width), bf16),
            pltpu.VMEM((CHUNKS, CHUNK, HEAD), bf16),
            pltpu.VMEM((tokens, 2 * HEAD), bf16),
            pltpu.VMEM((SEQS, SHARD, HEAD), bf16),
            pltpu.VMEM((SHARD, width), bf16),
            pltpu.VMEM((SHARD, width), bf16),
            dma((4,)),
            dma((len(GATHER),)),
            dma((SEQS,)),
            dma,
            dma((CHUNKS,)),
            dma((CHUNKS,)),
            dma((CHUNKS,)),
            dma((CHUNKS,)),
            dma,
            dma,
            dma,
            dma,
            dma((CHUNKS,)),
        ],
        compiler_params=pltpu.CompilerParams(
            collective_id=0, has_side_effects=True, vmem_limit_bytes=48 * 1024 * 1024
        ),
        name="sections",
    )(stream.reshape(CHUNKS, CHUNK, width), norm_gain, qkv_weight, out_weight, stale)
    return out, fresh.reshape(1, tokens, 1, 2 * HEAD)


def solution(mesh):
    return jax.shard_map(
        on_device,
        mesh=mesh,
        in_specs=(
            P(),
            P("sec", None),
            P("sec", None, "seq"),
            P("sec", "seq", None),
            P("sec", None, "seq", None),
        ),
        out_specs=(P("sec", "seq", None), P("sec", None, "seq", None)),
        check_vma=False,
    )
```
